512 devices in a mesh: tensor: 16 (over y, x), context: 32 (over z, core).
Axes of the slice: x: 4, y: 4, z: 16, core: 2. Of those that a mesh axis runs over, the one named last changes fastest.
Arguments:
- hidden: bfloat16 [8192, 2048], P('context', 'tensor'), may hold values from -6 to 6
- proj_qkvz: bfloat16 [2048, 12288], P(None, 'tensor'), may hold values from -0.125 to 0.125
- proj_rates: bfloat16 [2048, 64], P(None, 'tensor'), may hold values from -0.125 to 0.125
- conv_weight: float32 [4, 16, 512], P(None, 'tensor'), may hold values from -3 to 3
- decay_rate: float32 [32], P('tensor'), may hold values from 1e-05 to 0.1
- step_bias: float32 [32], P('tensor'), may hold values from -1 to 1
- norm_gain: float32 [128], replicated, may hold values from 0.5 to 1.5
- proj_out: bfloat16 [4096, 2048], P('tensor'), may hold values from -0.09375 to 0.09375
- doc_lengths: int32 [8], replicated, may hold values from 1 to 4096, 8192 in all
Outputs:
- layer_out: bfloat16 [8192, 2048], P('context', 'tensor')
The draws below stay inside these ranges and needn't reach their ends.
Inputs may be any that keep to these rules, and one draw needn't show every extreme that they name: `doc_lengths`: the lengths sum to 8192; the longest is exactly 4096.
All inputs are finite; a program needn't handle non-finite values.
Results may differ from the reference program's by a relative error of at most 0.02.
Values may be sent and summed in bfloat16 or wider, within the bound.
No kernel may reach another device: no remote copies, remote signals or barrier semaphores. Data moves between devices by JAX's collectives and lax.ppermute only.
A program may use at most 64 MiB of HBM per device.

```python
import math
import jax
import jax.numpy as jnp
import numpy as np
from jax import lax

D = 2048
NQK = 16
NV = 32
DK = 128
KERNEL = 4
DOCS = 8
SEQ = 8192


def block_scale(own_key, shape, split, smallest, high):
    def one(axis_at, shards_of):
        steps = jax.random.uniform(jax.random.fold_in(jax.random.fold_in(own_key, 6), axis_at), (shards_of,), jnp.float32, smallest / len(split), high / len(split))
        return jnp.repeat(jnp.exp(steps), shape[axis_at] // shards_of).reshape((-1,) + (1,) * (len(shape) - axis_at - 1))

    level = one(*split[0])
    for cut in split[1:]:
        level = level * one(*cut)
    return level


def length_profile(number_of, total, bound, slope):
    portions = [(1 << 20) // math.isqrt(rank ** slope) + 1 for rank in range(2, number_of + 1)]
    rest, counts = total - bound - (number_of - 1), [1] * (number_of - 1)
    while rest > 0:
        candidates = [i for i in range(number_of - 1) if counts[i] < bound]
        pool, left = sum([portions[i] for i in candidates]), rest
        for i in candidates:
            more = min(bound - counts[i], max(1, left * portions[i] // pool), rest)
            counts[i] = counts[i] + more
            rest = rest - more
    return np.array([bound] + counts)


def uneven_parts(key, number_of, total, limit, skew):
    if number_of == 2:
        one = jax.random.randint(key, (), max(1, total - limit), min(limit, total - 1) + 1)
        return jnp.stack([one, total - one])
    tallies = jnp.asarray(length_profile(number_of, total, limit, skew), jnp.int32)
    twos = (number_of - 1) // 2
    source_of, taker = tallies[1:1 + 2 * twos:2], tallies[2:2 + 2 * twos:2]
    room = jnp.minimum(source_of - 1, limit - taker)
    moved = jax.random.randint(jax.random.fold_in(key, 1), (twos,), 0, 1 << 20) % (room + 1)
    tallies = tallies.at[1:1 + 2 * twos:2].set(source_of - moved).at[2:2 + 2 * twos:2].set(taker + moved)
    return tallies[jax.random.permutation(jax.random.fold_in(key, 2), number_of)]


def bell_draw(stream_key, extent, scale, limit, split=(), held_as=jnp.bfloat16):
    array = scale * jax.random.normal(stream_key, extent, jnp.float32)
    if split:
        array = array * block_scale(stream_key, extent, split, -0.22, 0.18)
    return jnp.clip(array, -limit, limit).astype(held_as)


def setup_inputs(seed: int = 0) -> dict:
    splits = jax.random.split(jax.random.key(seed), 10)
    return {
        "hidden": bell_draw(splits[0], (SEQ, D), 1.0, 6.0, ((0, 32), (1, 16))),
        "proj_qkvz": bell_draw(splits[1], (D, NQK * 6 * DK), D ** -0.5, 0.125, ((1, 16),)),
        "proj_rates": bell_draw(splits[2], (D, NQK * 4), D ** -0.5, 0.125, ((1, 16),)),
        "conv_weight": bell_draw(splits[3], (KERNEL, NQK, 4 * DK), 0.5, 3.0, ((1, 16),), jnp.float32),
        "decay_rate": jnp.clip(jnp.exp(math.log(0.1) - 9.2103404 * jax.random.uniform(splits[4], (NV,), jnp.float32) ** block_scale(splits[4], (NV,), ((0, 16),), -0.2, 0.2)), 9.999999747378752e-06, 0.1),
        "step_bias": jnp.clip(jax.random.uniform(splits[5], (NV,), jnp.float32, -1.0, 1.0) * block_scale(splits[5], (NV,), ((0, 16),), -0.4, 0.0), -1.0, 1.0),
        "norm_gain": jnp.clip(1.0 + 0.1 * jax.random.normal(splits[6], (DK,), jnp.float32), 0.5, 1.5),
        "proj_out": bell_draw(splits[7], (NV * DK, D), (NV * DK) ** -0.5, 0.09375, ((0, 16),)),
        "doc_lengths": uneven_parts(splits[8], DOCS, SEQ, SEQ // 2, 2).astype(jnp.int32),
    }


PRECISE = lax.Precision.HIGHEST

def doc_index(positions, bounds):
    return lax.optimization_barrier(jnp.sum((bounds[None, :] <= positions[:, None]).astype(jnp.int32), axis=1))

def reference(hidden, proj_qkvz, proj_rates, conv_weight, decay_rate, step_bias, norm_gain, proj_out, doc_lengths):
    seq_len = hidden.shape[0]
    head_dim = norm_gain.shape[0]
    groups = proj_qkvz.shape[1] // (6 * head_dim)
    head_count = 2 * groups
    mixed = jnp.dot(hidden, proj_qkvz, preferred_element_type=jnp.float32).astype(jnp.bfloat16)
    mixed = mixed.reshape(seq_len, groups, 6 * head_dim)
    rates = jnp.dot(hidden, proj_rates, preferred_element_type=jnp.float32).astype(jnp.bfloat16)
    rates = rates.reshape(seq_len, groups, 4).astype(jnp.float32)
    bounds = jnp.cumsum(doc_lengths)[:-1].astype(jnp.int32)
    positions = jnp.arange(seq_len, dtype=jnp.int32)
    doc_ids = doc_index(positions, bounds)
    before = mixed[:, :, :4 * head_dim].astype(jnp.float32)
    convolved = jnp.zeros_like(before)
    for offset in range(KERNEL):
        shifted = jnp.concatenate([jnp.zeros((offset, groups, 4 * head_dim), jnp.float32), before[:seq_len - offset]], axis=0)
        keep_tap = (doc_index(positions - offset, bounds) == doc_ids).astype(jnp.float32)
        convolved = convolved + conv_weight[offset][None] * shifted * keep_tap[:, None, None]
    convolved = jax.nn.silu(convolved)
    query_vecs = convolved[:, :, :head_dim]
    key_vecs = convolved[:, :, head_dim:2 * head_dim]
    value_vecs = convolved[:, :, 2 * head_dim:].reshape(seq_len, head_count, head_dim)
    query_vecs = query_vecs / jnp.sqrt(lax.optimization_barrier(jnp.sum(query_vecs * query_vecs, -1, keepdims=True)) + 1e-06) / math.sqrt(head_dim)
    key_vecs = key_vecs / jnp.sqrt(lax.optimization_barrier(jnp.sum(key_vecs * key_vecs, -1, keepdims=True)) + 1e-06)
    beta_gate = jax.nn.sigmoid(rates[:, :, :2].reshape(seq_len, head_count))
    decays = -decay_rate[None] * jax.nn.softplus(rates[:, :, 2:].reshape(seq_len, head_count) + step_bias[None])
    same_prev = (doc_index(positions - 1, bounds) == doc_ids).astype(jnp.float32)
    alphas = jnp.exp(decays) * same_prev[:, None]

    def token_step(state_mat, inputs):
        query_row, key_row, value_row, beta_row, alpha_row = inputs
        query_head = jnp.repeat(query_row, 2, axis=0)
        key_head = jnp.repeat(key_row, 2, axis=0)
        recalled = jnp.einsum('hvk,hk->hv', state_mat, key_head, precision=PRECISE)
        update = jnp.einsum('hv,hk->hvk', value_row - alpha_row[:, None] * recalled, key_head, precision=PRECISE)
        state_mat = alpha_row[:, None, None] * state_mat + beta_row[:, None, None] * update
        return (state_mat, jnp.einsum('hvk,hk->hv', state_mat, query_head, precision=PRECISE))
    start_state = jnp.zeros((head_count, head_dim, head_dim), jnp.float32)
    _, outputs = lax.scan(token_step, start_state, (query_vecs, key_vecs, value_vecs, beta_gate, alphas))
    out_gate = mixed[:, :, 4 * head_dim:].reshape(seq_len, head_count, head_dim).astype(jnp.float32)
    rms_scale = lax.rsqrt(lax.optimization_barrier(jnp.mean(outputs * outputs, -1, keepdims=True)) + 1e-06)
    normed = (outputs * rms_scale * norm_gain * jax.nn.silu(out_gate)).astype(jnp.bfloat16)
    normed = normed.reshape(seq_len, head_count * head_dim)
    return jnp.dot(normed, proj_out, preferred_element_type=jnp.float32).astype(jnp.bfloat16)
```

```python
import functools
import math

import jax
import jax.numpy as jnp
from jax import lax
from jax.experimental import pallas as pl
from jax.experimental.pallas import tpu as pltpu
from jax.sharding import PartitionSpec as P

F32 = jnp.float32
BF16 = jnp.bfloat16
TAIL = 16
VMEM_LIMIT = 48 * 1024 * 1024


def mm(a, b):
    return jnp.dot(a.astype(BF16), b.astype(BF16), preferred_element_type=F32)


def mm_nt(a, b):
    return lax.dot_general(
        a.astype(BF16), b.astype(BF16), (((1,), (1,)), ((), ())), preferred_element_type=F32
    )


def halves(a):
    high = a.astype(BF16)
    return high, (a - high.astype(F32)).astype(BF16)


def mm3(a, b):
    a_high, a_low = halves(a)
    b_high, b_low = halves(b)
    return (
        jnp.dot(a_high, b_high, preferred_element_type=F32)
        + jnp.dot(a_high, b_low, preferred_element_type=F32)
        + jnp.dot(a_low, b_high, preferred_element_type=F32)
    )


def silu(v):
    return v / (1.0 + jnp.exp(-v))


def project_kernel(x_ref, w_ref, wr_ref, mixed_ref, rates_ref, wide):
    parts, _, width = x_ref.shape
    for part in range(parts):
        wide[:, part * width : (part + 1) * width] = x_ref[part]
    x = wide[...]
    mixed_ref[...] = jnp.dot(x, w_ref[...], preferred_element_type=F32).astype(BF16)
    rates_ref[...] = jnp.dot(x, wr_ref[...], preferred_element_type=F32).astype(BF16)


def unit_lower_inverses(lowers, rows_at, cols_at):
    rows = lowers[0].shape[0]
    eye = (rows_at == cols_at).astype(F32)

    def between(lower, size):
        joins = ((rows_at // (2 * size)) == (cols_at // (2 * size))) & (
            (rows_at // size) != (cols_at // size)
        )
        return jnp.where(joins, lower, 0.0)

    found = [eye - between(lower, 1) for lower in lowers]
    size = 2
    while size < rows:
        halfway = [mm3(between(lower, size), t) for lower, t in zip(lowers, found)]
        found = [t - mm3(t, h) for t, h in zip(found, halfway)]
        size *= 2
    return found


def chunk_kernel(
    lens_ref,
    first_ref,
    rate_ref,
    bias_ref,
    mixed_ref,
    rim_ref,
    rates_ref,
    cw_ref,
    c_ref,
    m_ref,
    o_ref,
    ext,
):
    rows = mixed_ref.shape[0]
    dk = cw_ref.shape[1] // 4
    first = first_ref[0]
    pos = first + lax.broadcasted_iota(jnp.int32, (rows, 1), 0)
    start = jnp.zeros((rows, 1), jnp.int32)
    bound = jnp.int32(0)
    for i in range(lens_ref.shape[0] - 1):
        bound = bound + lens_ref[i]
        start = jnp.where(pos >= bound, bound, start)

    ext[0:TAIL, :] = rim_ref[...].astype(F32)
    ext[TAIL : TAIL + rows, :] = mixed_ref[:, : 4 * dk].astype(F32)
    conv = cw_ref[0:1, :] * ext[TAIL : TAIL + rows, :]
    for j in range(1, 4):
        keep = (pos - j >= start).astype(F32)
        conv = conv + cw_ref[j : j + 1, :] * (ext[TAIL - j : TAIL - j + rows, :] * keep)
    conv = silu(conv)
    q = conv[:, :dk]
    k = conv[:, dk : 2 * dk]
    q = q * (lax.rsqrt(jnp.sum(q * q, -1, keepdims=True) + 1e-6) * (1.0 / math.sqrt(dk)))
    k = k * lax.rsqrt(jnp.sum(k * k, -1, keepdims=True) + 1e-6)
    qb = q.astype(BF16)
    kb = k.astype(BF16)

    rates = rates_ref[...].astype(F32)
    betas = 1.0 / (1.0 + jnp.exp(-rates[:, 0:2]))
    lane2 = lax.broadcasted_iota(jnp.int32, (1, 2), 1)
    bias = jnp.where(lane2 == 0, bias_ref[0], bias_ref[1])
    decay = jnp.where(lane2 == 0, rate_ref[0], rate_ref[1])
    a_in = rates[:, 2:4] + bias
    steps = -decay * (jnp.maximum(a_in, 0.0) + jnp.log1p(jnp.exp(-jnp.abs(a_in))))

    rows_at = lax.broadcasted_iota(jnp.int32, (rows, rows), 0)
    cols_at = lax.broadcasted_iota(jnp.int32, (rows, rows), 1)
    lower = rows_at >= cols_at
    tri = lower.astype(BF16)
    lanes = lax.broadcasted_iota(jnp.int32, (1, dk), 1)
    padded = jnp.where(lanes == 0, steps[:, 0:1], jnp.where(lanes == 1, steps[:, 1:2], 0.0))
    p1 = padded.astype(BF16)
    r1 = padded - p1.astype(F32)
    p2 = r1.astype(BF16)
    p3 = (r1 - p2.astype(F32)).astype(BF16)
    cumul = (
        jnp.dot(tri, p1, preferred_element_type=F32)
        + jnp.dot(tri, p2, preferred_element_type=F32)
        + jnp.dot(tri, p3, preferred_element_type=F32)
    )
    cumul_t = jnp.transpose(cumul)

    visible = lower & (cols_at + first >= start)
    gram = mm_nt(kb, kb)
    cross = mm_nt(qb, kb)
    last_start = start[rows - 1 : rows, :]
    carries = (start < first).astype(F32)
    in_tail = (pos >= last_start).astype(F32)

    lowers, scores = [], []
    for h in range(2):
        differ = cumul[:, h : h + 1] - cumul_t[h : h + 1, :]
        ratio = jnp.where(visible, jnp.exp(jnp.where(visible, differ, 0.0)), 0.0)
        scores.append(cross * ratio)
        lowers.append(
            jnp.where(rows_at > cols_at, betas[:, h : h + 1] * ratio * gram, 0.0)
        )
    inverses = unit_lower_inverses(lowers, rows_at, cols_at)
    square = lax.broadcasted_iota(jnp.int32, (dk, 2 * dk), 0)
    across = lax.broadcasted_iota(jnp.int32, (dk, 2 * dk), 1)
    for h in range(2):
        col = cumul[:, h : h + 1]
        beta = betas[:, h : h + 1]
        gamma = jnp.exp(col) * carries
        value = conv[:, (2 + h) * dk : (3 + h) * dk]
        rhs = jnp.concatenate([(beta * gamma) * k, beta * value], axis=1)
        wu = mm(inverses[h], rhs)
        last = col[rows - 1 : rows, :]
        tail = jnp.exp(last - col) * in_tail
        k_tail = jnp.transpose(k * tail)
        made = mm(k_tail, wu)
        gamma_last = gamma[rows - 1 : rows, :]
        c_ref[h] = (
            jnp.where(square == across, gamma_last, 0.0) + jnp.where(across < dk, -made, made)
        ).astype(BF16)
        both = mm(scores[h], wu)
        m_ref[h] = (gamma * q - both[:, :dk]).astype(BF16)
        o_ref[h] = both[:, dk:]


def compose(late, early):
    dk = late.shape[0]
    made = jnp.dot(late[:, :dk], early, preferred_element_type=F32)
    across = lax.broadcasted_iota(jnp.int32, made.shape, 1)
    return made + jnp.where(across < dk, 0.0, late.astype(F32))


def compose_kernel(late_ref, early_ref, out_ref):
    for h in range(2):
        out_ref[h] = compose(late_ref[h], early_ref[h]).astype(BF16)


def finish_kernel(near_ref, far_ref, m_ref, o_ref, gate_ref, gain_ref, w_ref, out_ref):
    dk = gain_ref.shape[1]
    parts, _, width = out_ref.shape
    sides = []
    for h in range(2):
        near = near_ref[h]
        state = jnp.dot(near[:, :dk], far_ref[h], preferred_element_type=F32)
        state = state + near[:, dk:].astype(F32)
        rec = o_ref[h] + jnp.dot(m_ref[h], state.astype(BF16), preferred_element_type=F32)
        scale = lax.rsqrt(jnp.mean(rec * rec, -1, keepdims=True) + 1e-6)
        gate = silu(gate_ref[:, h * dk : (h + 1) * dk].astype(F32))
        sides.append((rec * scale * gain_ref[...] * gate).astype(BF16))
    normed = jnp.concatenate(sides, axis=1)
    share = jnp.dot(normed, w_ref[...], preferred_element_type=F32).astype(BF16)
    for part in range(parts):
        out_ref[part] = share[:, part * width : (part + 1) * width]


def vmem():
    return pl.BlockSpec(memory_space=pltpu.VMEM)


def smem():
    return pl.BlockSpec(memory_space=pltpu.SMEM)


def params():
    return pltpu.CompilerParams(vmem_limit_bytes=VMEM_LIMIT)


def shifted(array, by):
    peers = lax.axis_size("context")
    return lax.ppermute(array, "context", [(i, i + by) for i in range(peers - by)])


def local(
    hidden,
    proj_qkvz,
    proj_rates,
    conv_weight,
    decay_rate,
    step_bias,
    norm_gain,
    proj_out,
    doc_lengths,
):
    rows, width = hidden.shape
    dk = norm_gain.shape[0]
    peers = lax.axis_size("tensor")
    first = (lax.axis_index("context") * rows).astype(jnp.int32).reshape(1)
    shape = jax.ShapeDtypeStruct

    spread = jnp.broadcast_to(hidden[None], (peers, rows, width))
    gathered = lax.all_to_all(spread, "tensor", 0, 0, tiled=True)
    mixed, rates = pl.pallas_call(
        project_kernel,
        out_shape=(shape((rows, 6 * dk), BF16), shape((rows, 4), BF16)),
        in_specs=[vmem()] * 3,
        out_specs=(vmem(), vmem()),
        scratch_shapes=[pltpu.VMEM((rows, peers * width), BF16)],
        compiler_params=params(),
    )(gathered, proj_qkvz, proj_rates)
    rim = shifted(mixed[rows - TAIL :, : 4 * dk], 1)

    summary, follow, own = pl.pallas_call(
        chunk_kernel,
        out_shape=(
            shape((2, dk, 2 * dk), BF16),
            shape((2, rows, dk), BF16),
            shape((2, rows, dk), F32),
        ),
        in_specs=[smem()] * 4 + [vmem()] * 4,
        out_specs=(vmem(), vmem(), vmem()),
        scratch_shapes=[pltpu.VMEM((rows + TAIL, 4 * dk), F32)],
        compiler_params=params(),
    )(
        doc_lengths,
        first,
        decay_rate,
        step_bias,
        mixed,
        rim,
        rates,
        conv_weight.reshape(4, 4 * dk),
    )

    def joined(late, early):
        return pl.pallas_call(
            compose_kernel,
            out_shape=shape((2, dk, 2 * dk), BF16),
            in_specs=[vmem()] * 2,
            out_specs=vmem(),
            compiler_params=params(),
        )(late, early)

    window = joined(shifted(summary, 1), shifted(summary, 2))
    window = joined(window, shifted(window, 2))
    window = joined(window, shifted(window, 4))
    far = shifted(window[:, :, dk:], 8)

    share = pl.pallas_call(
        finish_kernel,
        out_shape=shape((peers, rows, width), BF16),
        in_specs=[vmem()] * 7,
        out_specs=vmem(),
        compiler_params=params(),
    )(window, far, follow, own, mixed[:, 4 * dk :], norm_gain.reshape(1, dk), proj_out)
    shares = lax.all_to_all(share, "tensor", 0, 0, tiled=True)
    return jnp.sum(shares.astype(F32), axis=0).astype(BF16)


def solution(mesh):
    placed = (
        P("context", "tensor"),
        P(None, "tensor"),
        P(None, "tensor"),
        P(None, "tensor", None),
        P("tensor"),
        P("tensor"),
        P(),
        P("tensor", None),
        P(),
    )
    return jax.shard_map(
        local, mesh=mesh, in_specs=placed, out_specs=P("context", "tensor"), check_vma=False
    )
```

```python
import functools
import math

import jax
import jax.numpy as jnp
from jax import lax
from jax.experimental import pallas as pl
from jax.experimental.pallas import tpu as pltpu
from jax.sharding import PartitionSpec as P

F32 = jnp.float32
BF16 = jnp.bfloat16
TAIL = 16
VMEM_LIMIT = 48 * 1024 * 1024


def mm(a, b):
    return jnp.dot(a.astype(BF16), b.astype(BF16), preferred_element_type=F32)


def mm_nt(a, b):
    return lax.dot_general(
        a.astype(BF16), b.astype(BF16), (((1,), (1,)), ((), ())), preferred_element_type=F32
    )


def silu(v):
    return v / (1.0 + jnp.exp(-v))


def spread_kernel(x_ref, rim_ref, out_ref):
    block = x_ref[...]
    rim = rim_ref[...]
    for part in range(out_ref.shape[0]):
        out_ref[part, 0:TAIL, :] = rim
        out_ref[part, TAIL:, :] = block


def stage_kernel(w_ref, out_ref, sem):
    copy = pltpu.make_async_copy(w_ref, out_ref, sem)
    copy.start()
    copy.wait()


def unit_lower_inverses(lowers, rows_at, cols_at):
    rows = lowers[0].shape[0]
    eye = (rows_at == cols_at).astype(F32)

    def between(lower, size):
        joins = ((rows_at // (2 * size)) == (cols_at // (2 * size))) & (
            (rows_at // size) != (cols_at // size)
        )
        return jnp.where(joins, lower, 0.0)

    found = [eye - between(lower, 1) for lower in lowers]
    size = 2
    while size < rows:
        halfway = [mm(between(lower, size), t) for lower, t in zip(lowers, found)]
        found = [t - mm(t, h) for t, h in zip(found, halfway)]
        size *= 2
    return found


def chunk_kernel(
    lens_ref,
    first_ref,
    rate_ref,
    bias_ref,
    x_ref,
    w_ref,
    wr_ref,
    cw_ref,
    c_ref,
    m_ref,
    o_ref,
    z_ref,
    wide,
    ext,
):
    parts, rows, width = x_ref.shape
    rows = rows - TAIL
    dk = cw_ref.shape[2] // 4
    for part in range(parts):
        wide[:, part * width : (part + 1) * width] = x_ref[part]
    mixed = jnp.dot(wide[...], w_ref[...], preferred_element_type=F32)
    ext[...] = mixed[:, : 4 * dk].astype(BF16).astype(F32)
    z_ref[...] = mixed[TAIL : TAIL + rows, 4 * dk :].astype(BF16)
    rates = mm_nt(wide[TAIL : TAIL + rows, :], wr_ref[...]).astype(BF16).astype(F32)
    first = first_ref[0]
    pos = first + lax.broadcasted_iota(jnp.int32, (rows, 1), 0)
    start = jnp.zeros((rows, 1), jnp.int32)
    bound = jnp.int32(0)
    for i in range(lens_ref.shape[0] - 1):
        bound = bound + lens_ref[i]
        start = jnp.where(pos >= bound, bound, start)

    conv = cw_ref[0] * ext[TAIL : TAIL + rows, :]
    for j in range(1, 4):
        keep = (pos - j >= start).astype(F32)
        conv = conv + cw_ref[j] * (ext[TAIL - j : TAIL - j + rows, :] * keep)
    conv = silu(conv)
    q = conv[:, :dk]
    k = conv[:, dk : 2 * dk]
    q = q * (lax.rsqrt(jnp.sum(q * q, -1, keepdims=True) + 1e-6) * (1.0 / math.sqrt(dk)))
    k = k * lax.rsqrt(jnp.sum(k * k, -1, keepdims=True) + 1e-6)
    qb = q.astype(BF16)
    kb = k.astype(BF16)

    betas = 1.0 / (1.0 + jnp.exp(-rates[:, 0:2]))
    lane2 = lax.broadcasted_iota(jnp.int32, (1, 2), 1)
    bias = jnp.where(lane2 == 0, bias_ref[0], bias_ref[1])
    decay = jnp.where(lane2 == 0, rate_ref[0], rate_ref[1])
    a_in = rates[:, 2:4] + bias
    steps = -decay * (jnp.maximum(a_in, 0.0) + jnp.log1p(jnp.exp(-jnp.abs(a_in))))

    rows_at = lax.broadcasted_iota(jnp.int32, (rows, rows), 0)
    cols_at = lax.broadcasted_iota(jnp.int32, (rows, rows), 1)
    lower = rows_at >= cols_at
    tri = lower.astype(BF16)
    lanes = lax.broadcasted_iota(jnp.int32, (1, dk), 1)
    padded = jnp.where(lanes == 0, steps[:, 0:1], jnp.where(lanes == 1, steps[:, 1:2], 0.0))
    p1 = padded.astype(BF16)
    r1 = padded - p1.astype(F32)
    p2 = r1.astype(BF16)
    p3 = (r1 - p2.astype(F32)).astype(BF16)
    cumul = (
        jnp.dot(tri, p1, preferred_element_type=F32)
        + jnp.dot(tri, p2, preferred_element_type=F32)
        + jnp.dot(tri, p3, preferred_element_type=F32)
    )
    cumul_t = jnp.transpose(cumul)

    visible = lower & (cols_at + first >= start)
    gram = mm_nt(kb, kb)
    cross = mm_nt(qb, kb)
    last_start = start[rows - 1 : rows, :]
    carries = (start < first).astype(F32)
    in_tail = (pos >= last_start).astype(F32)

    lowers, scores = [], []
    for h in range(2):
        differ = cumul[:, h : h + 1] - cumul_t[h : h + 1, :]
        ratio = jnp.where(visible, jnp.exp(jnp.where(visible, differ, 0.0)), 0.0)
        scores.append(cross * ratio)
        lowers.append(
            jnp.where(rows_at > cols_at, betas[:, h : h + 1] * ratio * gram, 0.0)
        )
    inverses = unit_lower_inverses(lowers, rows_at, cols_at)
    square = lax.broadcasted_iota(jnp.int32, (dk, 2 * dk), 0)
    across = lax.broadcasted_iota(jnp.int32, (dk, 2 * dk), 1)
    for h in range(2):
        col = cumul[:, h : h + 1]
        beta = betas[:, h : h + 1]
        gamma = jnp.exp(col) * carries
        value = conv[:, (2 + h) * dk : (3 + h) * dk]
        rhs = jnp.concatenate([(beta * gamma) * k, beta * value], axis=1)
        wu = mm(inverses[h], rhs)
        last = col[rows - 1 : rows, :]
        tail = jnp.exp(last - col) * in_tail
        k_tail = jnp.transpose(k * tail)
        made = mm(k_tail, wu)
        gamma_last = gamma[rows - 1 : rows, :]
        c_ref[h] = (
            jnp.where(square == across, gamma_last, 0.0) + jnp.where(across < dk, -made, made)
        ).astype(BF16)
        both = mm(scores[h], wu)
        m_ref[h] = (gamma * q - both[:, :dk]).astype(BF16)
        o_ref[h] = both[:, dk:]


def compose(late, early):
    dk = late.shape[0]
    made = jnp.dot(late[:, :dk], early, preferred_element_type=F32)
    across = lax.broadcasted_iota(jnp.int32, made.shape, 1)
    return made + jnp.where(across < dk, 0.0, late.astype(F32))


def compose_kernel(late_ref, early_ref, out_ref):
    for h in range(2):
        out_ref[h] = compose(late_ref[h], early_ref[h]).astype(BF16)


def finish_kernel(near_ref, far_ref, m_ref, o_ref, gate_ref, gain_ref, w_ref, out_ref):
    dk = gain_ref.shape[1]
    parts, _, width = out_ref.shape
    sides = []
    for h in range(2):
        near = near_ref[h]
        state = jnp.dot(near[:, :dk], far_ref[h], preferred_element_type=F32)
        state = state + near[:, dk:].astype(F32)
        rec = o_ref[h] + jnp.dot(m_ref[h], state.astype(BF16), preferred_element_type=F32)
        scale = lax.rsqrt(jnp.mean(rec * rec, -1, keepdims=True) + 1e-6)
        gate = silu(gate_ref[:, h * dk : (h + 1) * dk].astype(F32))
        sides.append((rec * scale * gain_ref[...] * gate).astype(BF16))
    normed = jnp.concatenate(sides, axis=1)
    share = jnp.dot(normed, w_ref[...], preferred_element_type=F32).astype(BF16)
    for part in range(parts):
        out_ref[part] = share[:, part * width : (part + 1) * width]


def vmem():
    return pl.BlockSpec(memory_space=pltpu.VMEM)


def smem():
    return pl.BlockSpec(memory_space=pltpu.SMEM)


def params():
    return pltpu.CompilerParams(vmem_limit_bytes=VMEM_LIMIT)


def shifted(array, by):
    peers = lax.axis_size("context")
    return lax.ppermute(array, "context", [(i, i + by) for i in range(peers - by)])


def local(
    hidden,
    proj_qkvz,
    proj_rates,
    conv_weight,
    decay_rate,
    step_bias,
    norm_gain,
    proj_out,
    doc_lengths,
):
    rows, width = hidden.shape
    dk = norm_gain.shape[0]
    peers = lax.axis_size("tensor")
    first = (lax.axis_index("context") * rows).astype(jnp.int32).reshape(1)
    shape = jax.ShapeDtypeStruct

    tail = shifted(hidden[rows - TAIL :], 1)
    spread = pl.pallas_call(
        spread_kernel,
        out_shape=shape((peers, TAIL + rows, width), BF16),
        in_specs=[vmem()] * 2,
        out_specs=vmem(),
        compiler_params=params(),
    )(hidden, tail)
    staged = pl.pallas_call(
        stage_kernel,
        out_shape=shape(proj_qkvz.shape, BF16),
        in_specs=[pl.BlockSpec(memory_space=pl.ANY)],
        out_specs=vmem(),
        scratch_shapes=[pltpu.SemaphoreType.DMA],
        compiler_params=params(),
    )(proj_qkvz)
    spread, staged, first = lax.optimization_barrier((spread, staged, first))
    gathered = lax.all_to_all(spread, "tensor", 0, 0, tiled=True)

    summary, follow, own, gate = pl.pallas_call(
        chunk_kernel,
        out_shape=(
            shape((2, dk, 2 * dk), BF16),
            shape((2, rows, dk), BF16),
            shape((2, rows, dk), F32),
            shape((rows, 2 * dk), BF16),
        ),
        in_specs=[smem()] * 4 + [vmem()] * 4,
        out_specs=(vmem(),) * 4,
        scratch_shapes=[
            pltpu.VMEM((rows + TAIL, peers * width), BF16),
            pltpu.VMEM((rows + TAIL, 4 * dk), F32),
        ],
        compiler_params=params(),
    )(
        doc_lengths,
        first,
        decay_rate,
        step_bias,
        gathered,
        staged,
        proj_rates.T,
        conv_weight,
    )

    def joined(late, early):
        return pl.pallas_call(
            compose_kernel,
            out_shape=shape((2, dk, 2 * dk), BF16),
            in_specs=[vmem()] * 2,
            out_specs=vmem(),
            compiler_params=params(),
        )(late, early)

    window = joined(shifted(summary, 1), shifted(summary, 2))
    window = joined(window, shifted(window, 2))
    window = joined(window, shifted(window, 4))
    far = shifted(window[:, :, dk:], 8)

    share = pl.pallas_call(
        finish_kernel,
        out_shape=shape((peers, rows, width), BF16),
        in_specs=[vmem()] * 7,
        out_specs=vmem(),
        compiler_params=params(),
    )(window, far, follow, own, gate, norm_gain.reshape(1, dk), proj_out)
    shares = lax.all_to_all(share, "tensor", 0, 0, tiled=True)
    return jnp.sum(shares.astype(F32), axis=0).astype(BF16)


def solution(mesh):
    placed = (
        P("context", "tensor"),
        P(None, "tensor"),
        P(None, "tensor"),
        P(None, "tensor", None),
        P("tensor"),
        P("tensor"),
        P(),
        P("tensor", None),
        P(),
    )
    return jax.shard_map(
        local, mesh=mesh, in_specs=placed, out_specs=P("context", "tensor"), check_vma=False
    )
```

```python
import functools
import math

import jax
import jax.numpy as jnp
from jax import lax
from jax.experimental import pallas as pl
from jax.experimental.pallas import tpu as pltpu
from jax.sharding import PartitionSpec as P

F32 = jnp.float32
BF16 = jnp.bfloat16
TAIL = 16
VMEM_LIMIT = 48 * 1024 * 1024


def mm(a, b):
    return jnp.dot(a.astype(BF16), b.astype(BF16), preferred_element_type=F32)


def mm_nt(a, b):
    return lax.dot_general(
        a.astype(BF16), b.astype(BF16), (((1,), (1,)), ((), ())), preferred_element_type=F32
    )


def silu(v):
    return v / (1.0 + jnp.exp(-v))


def spread_kernel(x_ref, rim_ref, out_ref):
    block = x_ref[...]
    rim = rim_ref[...]
    for part in range(out_ref.shape[0]):
        out_ref[part, 0:TAIL, :] = rim
        out_ref[part, TAIL:, :] = block


def stage_kernel(w_ref, out_ref, sem):
    copy = pltpu.make_async_copy(w_ref, out_ref, sem)
    copy.start()
    copy.wait()


def unit_lower_inverses(lowers, rows_at, cols_at):
    rows = lowers[0].shape[0]
    eye = (rows_at == cols_at).astype(F32)

    def joins(size):
        together = (rows_at // (2 * size)) == (cols_at // (2 * size))
        return together & ((rows_at // size) != (cols_at // size))

    first = joins(1)
    found = [eye - jnp.where(first, lower, 0.0) for lower in lowers]
    size = 2
    while size < rows:
        mask = joins(size)
        halfway = [mm(jnp.where(mask, lower, 0.0), t) for lower, t in zip(lowers, found)]
        found = [t - mm(t, h) for t, h in zip(found, halfway)]
        size *= 2
    return found


def chunk_kernel(
    lens_ref,
    first_ref,
    rate_ref,
    bias_ref,
    x_ref,
    w_ref,
    wr_ref,
    cw_ref,
    c_ref,
    wu_ref,
    ratio_ref,
    q_ref,
    k_ref,
    follow_ref,
    wide,
    ext,
):
    parts, rows, width = x_ref.shape
    rows = rows - TAIL
    dk = cw_ref.shape[2] // 4
    for part in range(parts):
        wide[:, part * width : (part + 1) * width] = x_ref[part]
    mixed = jnp.dot(wide[...], w_ref[:, : 4 * dk], preferred_element_type=F32)
    ext[...] = mixed.astype(BF16).astype(F32)
    rates = mm_nt(wide[TAIL : TAIL + rows, :], wr_ref[...]).astype(BF16).astype(F32)
    first = first_ref[0]
    pos = first + lax.broadcasted_iota(jnp.int32, (rows, 1), 0)
    start = jnp.zeros((rows, 1), jnp.int32)
    bound = jnp.int32(0)
    for i in range(lens_ref.shape[0] - 1):
        bound = bound + lens_ref[i]
        start = jnp.where(pos >= bound, bound, start)

    conv = cw_ref[0] * ext[TAIL : TAIL + rows, :]
    for j in range(1, 4):
        keep = (pos - j >= start).astype(F32)
        conv = conv + cw_ref[j] * (ext[TAIL - j : TAIL - j + rows, :] * keep)
    conv = silu(conv)
    q = conv[:, :dk]
    k = conv[:, dk : 2 * dk]
    q = q * (lax.rsqrt(jnp.sum(q * q, -1, keepdims=True) + 1e-6) * (1.0 / math.sqrt(dk)))
    k = k * lax.rsqrt(jnp.sum(k * k, -1, keepdims=True) + 1e-6)
    qb = q.astype(BF16)
    kb = k.astype(BF16)

    betas = 1.0 / (1.0 + jnp.exp(-rates[:, 0:2]))
    lane2 = lax.broadcasted_iota(jnp.int32, (1, 2), 1)
    bias = jnp.where(lane2 == 0, bias_ref[0], bias_ref[1])
    decay = jnp.where(lane2 == 0, rate_ref[0], rate_ref[1])
    a_in = rates[:, 2:4] + bias
    steps = -decay * (jnp.maximum(a_in, 0.0) + jnp.log1p(jnp.exp(-jnp.abs(a_in))))

    rows_at = lax.broadcasted_iota(jnp.int32, (rows, rows), 0)
    cols_at = lax.broadcasted_iota(jnp.int32, (rows, rows), 1)
    lower = rows_at >= cols_at
    tri = lower.astype(BF16)
    lanes = lax.broadcasted_iota(jnp.int32, (1, dk), 1)
    padded = jnp.where(lanes == 0, steps[:, 0:1], jnp.where(lanes == 1, steps[:, 1:2], 0.0))
    p1 = padded.astype(BF16)
    r1 = padded - p1.astype(F32)
    p2 = r1.astype(BF16)
    p3 = (r1 - p2.astype(F32)).astype(BF16)
    cumul = (
        jnp.dot(tri, p1, preferred_element_type=F32)
        + jnp.dot(tri, p2, preferred_element_type=F32)
        + jnp.dot(tri, p3, preferred_element_type=F32)
    )
    cumul_t = jnp.transpose(cumul)

    visible = lower & (cols_at + first >= start)
    gram = mm_nt(kb, kb)
    last_start = start[rows - 1 : rows, :]
    carries = (start < first).astype(F32)
    in_tail = (pos >= last_start).astype(F32)
    q_ref[...] = qb
    k_ref[...] = kb

    half = rows // 2
    diagonals, below, rights = [], [], []
    for h in range(2):
        col = cumul[:, h : h + 1]
        beta = betas[:, h : h + 1]
        gamma = jnp.exp(col) * carries
        differ = col - cumul_t[h : h + 1, :]
        ratio = jnp.where(visible, jnp.exp(jnp.where(visible, differ, 0.0)), 0.0)
        ratio_ref[h] = ratio
        weighed = beta * ratio * gram
        diagonals.append(weighed[:half, :half])
        diagonals.append(weighed[half:, half:])
        below.append(weighed[half:, :half])
        value = conv[:, (2 + h) * dk : (3 + h) * dk]
        rights.append(jnp.concatenate([(beta * gamma) * k, beta * value], axis=1))
        follow_ref[h] = (gamma * q).astype(BF16)
    inverses = unit_lower_inverses(
        diagonals, rows_at[:half, :half], cols_at[:half, :half]
    )
    tops = [mm(inverses[2 * h], rights[h][:half]) for h in range(2)]
    reduced = [rights[h][half:] - mm(below[h], tops[h]) for h in range(2)]
    bottoms = [mm(inverses[2 * h + 1], reduced[h]) for h in range(2)]
    square = lax.broadcasted_iota(jnp.int32, (dk, 2 * dk), 0)
    across = lax.broadcasted_iota(jnp.int32, (dk, 2 * dk), 1)
    for h in range(2):
        col = cumul[:, h : h + 1]
        last = col[rows - 1 : rows, :]
        k_tail = jnp.transpose(k * (jnp.exp(last - col) * in_tail)).astype(BF16)
        wu = jnp.concatenate([tops[h], bottoms[h]], axis=0).astype(BF16)
        wu_ref[h] = wu
        made = jnp.dot(k_tail, wu, preferred_element_type=F32)
        gamma_last = jnp.exp(last) * carries[rows - 1 : rows, :]
        c_ref[h] = (
            jnp.where(square == across, gamma_last, 0.0) + jnp.where(across < dk, -made, made)
        ).astype(BF16)


def detail_kernel(
    x_ref, w_ref, wu_ref, ratio_ref, q_ref, k_ref, follow_ref, gain_ref, m_ref, o_ref, gate_ref, wide
):
    parts, rows, width = x_ref.shape
    rows = rows - TAIL
    dk = gain_ref.shape[1]
    cross = mm_nt(q_ref[...], k_ref[...])
    for h in range(2):
        both = mm(cross * ratio_ref[h], wu_ref[h])
        m_ref[h] = (follow_ref[h].astype(F32) - both[:, :dk]).astype(BF16)
        o_ref[h] = both[:, dk:]
    for part in range(parts):
        wide[:, part * width : (part + 1) * width] = x_ref[part, TAIL : TAIL + rows, :]
    z = jnp.dot(wide[...], w_ref[:, 4 * dk :], preferred_element_type=F32)
    gate = silu(z.astype(BF16).astype(F32))
    for h in range(2):
        gate_ref[:, h * dk : (h + 1) * dk] = gate[:, h * dk : (h + 1) * dk] * gain_ref[...]


def compose(late, early):
    dk = late.shape[0]
    made = jnp.dot(late[:, :dk], early, preferred_element_type=F32)
    across = lax.broadcasted_iota(jnp.int32, made.shape, 1)
    return made + jnp.where(across < dk, 0.0, late.astype(F32))


def compose_kernel(late_ref, early_ref, out_ref):
    for h in range(2):
        out_ref[h] = compose(late_ref[h], early_ref[h]).astype(BF16)


def advance(summary, state):
    dk = summary.shape[0]
    moved = jnp.dot(summary[:, :dk], state, preferred_element_type=F32)
    return (moved + summary[:, dk:].astype(F32)).astype(BF16)


def enter_kernel(near_ref, far_ref, out_ref):
    for h in range(2):
        out_ref[h] = advance(near_ref[h], far_ref[h])


def finish_kernel(
    made_ref, given_ref, first_half_ref, m_ref, o_ref, gate_ref, w_ref, out_ref
):
    dk = m_ref.shape[2]
    parts, _, width = out_ref.shape
    sides = []
    for h in range(2):
        state = given_ref[h] + advance(first_half_ref[h], made_ref[h])
        rec = o_ref[h] + jnp.dot(m_ref[h], state, preferred_element_type=F32)
        scale = lax.rsqrt(jnp.mean(rec * rec, -1, keepdims=True) + 1e-6)
        sides.append((rec * scale * gate_ref[:, h * dk : (h + 1) * dk]).astype(BF16))
    normed = jnp.concatenate(sides, axis=1)
    share = jnp.dot(normed, w_ref[...], preferred_element_type=F32).astype(BF16)
    for part in range(parts):
        out_ref[part] = share[:, part * width : (part + 1) * width]


def vmem():
    return pl.BlockSpec(memory_space=pltpu.VMEM)


def smem():
    return pl.BlockSpec(memory_space=pltpu.SMEM)


def params():
    return pltpu.CompilerParams(vmem_limit_bytes=VMEM_LIMIT)


def shifted(array, by):
    peers = lax.axis_size("context")
    return lax.ppermute(array, "context", [(i, i + by) for i in range(peers - by)])


def within_chip(array, source):
    peers = lax.axis_size("context")
    pairs = [(i + source, i + 1 - source) for i in range(0, peers, 2)]
    return lax.ppermute(array, "context", pairs)


def over_chips(array, by):
    peers = lax.axis_size("context")
    pairs = [(i, i + 2 * by) for i in range(1, peers - 2 * by, 2)]
    return lax.ppermute(array, "context", pairs)


def local(
    hidden,
    proj_qkvz,
    proj_rates,
    conv_weight,
    decay_rate,
    step_bias,
    norm_gain,
    proj_out,
    doc_lengths,
):
    rows, width = hidden.shape
    dk = norm_gain.shape[0]
    peers = lax.axis_size("tensor")
    first = (lax.axis_index("context") * rows).astype(jnp.int32).reshape(1)
    shape = jax.ShapeDtypeStruct

    tail = shifted(hidden[rows - TAIL :], 1)
    spread = pl.pallas_call(
        spread_kernel,
        out_shape=shape((peers, TAIL + rows, width), BF16),
        in_specs=[vmem()] * 2,
        out_specs=vmem(),
        compiler_params=params(),
    )(hidden, tail)
    staged = pl.pallas_call(
        stage_kernel,
        out_shape=shape(proj_qkvz.shape, BF16),
        in_specs=[pl.BlockSpec(memory_space=pl.ANY)],
        out_specs=vmem(),
        scratch_shapes=[pltpu.SemaphoreType.DMA],
        compiler_params=params(),
    )(proj_qkvz)
    spread, staged, first = lax.optimization_barrier((spread, staged, first))
    gathered = lax.all_to_all(spread, "tensor", 0, 0, tiled=True)

    summary, inner, ratio, query, key, reach = pl.pallas_call(
        chunk_kernel,
        out_shape=(
            shape((2, dk, 2 * dk), BF16),
            shape((2, rows, 2 * dk), BF16),
            shape((2, rows, rows), F32),
            shape((rows, dk), BF16),
            shape((rows, dk), BF16),
            shape((2, rows, dk), BF16),
        ),
        in_specs=[smem()] * 4 + [vmem()] * 4,
        out_specs=(vmem(),) * 6,
        scratch_shapes=[
            pltpu.VMEM((rows + TAIL, peers * width), BF16),
            pltpu.VMEM((rows + TAIL, 4 * dk), F32),
        ],
        compiler_params=params(),
    )(
        doc_lengths,
        first,
        decay_rate,
        step_bias,
        gathered,
        staged,
        proj_rates.T,
        conv_weight,
    )
    follow, own, gate = pl.pallas_call(
        detail_kernel,
        out_shape=(
            shape((2, rows, dk), BF16),
            shape((2, rows, dk), F32),
            shape((rows, 2 * dk), F32),
        ),
        in_specs=[vmem()] * 8,
        out_specs=(vmem(),) * 3,
        scratch_shapes=[pltpu.VMEM((rows, peers * width), BF16)],
        compiler_params=params(),
    )(gathered, staged, inner, ratio, query, key, reach, norm_gain.reshape(1, dk))

    def small(kernel, columns, *arrays):
        return pl.pallas_call(
            kernel,
            out_shape=shape((2, dk, columns), BF16),
            in_specs=[vmem()] * len(arrays),
            out_specs=vmem(),
            compiler_params=params(),
        )(*arrays)

    first_half = within_chip(summary, 0)
    first_half, follow, own, gate = lax.optimization_barrier((first_half, follow, own, gate))
    chip = small(compose_kernel, 2 * dk, summary, first_half)
    window = small(compose_kernel, 2 * dk, over_chips(chip, 1), over_chips(chip, 2))
    window = small(compose_kernel, 2 * dk, window, over_chips(window, 2))
    made = small(enter_kernel, dk, window, over_chips(window[:, :, dk:], 4))
    given = within_chip(made, 1)

    share = pl.pallas_call(
        finish_kernel,
        out_shape=shape((peers, rows, width), BF16),
        in_specs=[vmem()] * 7,
        out_specs=vmem(),
        compiler_params=params(),
    )(made, given, first_half, follow, own, gate, proj_out)
    shares = lax.all_to_all(share, "tensor", 0, 0, tiled=True)
    return jnp.sum(shares.astype(F32), axis=0).astype(BF16)


def solution(mesh):
    placed = (
        P("context", "tensor"),
        P(None, "tensor"),
        P(None, "tensor"),
        P(None, "tensor", None),
        P("tensor"),
        P("tensor"),
        P(),
        P("tensor", None),
        P(),
    )
    return jax.shard_map(
        local, mesh=mesh, in_specs=placed, out_specs=P("context", "tensor"), check_vma=False
    )
```

```python
import functools
import math

import jax
import jax.numpy as jnp
from jax import lax
from jax.experimental import pallas as pl
from jax.experimental.pallas import tpu as pltpu
from jax.sharding import PartitionSpec as P

F32 = jnp.float32
BF16 = jnp.bfloat16
TAIL = 16
VMEM_LIMIT = 48 * 1024 * 1024


def mm(a, b):
    return jnp.dot(a.astype(BF16), b.astype(BF16), preferred_element_type=F32)


def mm_nt(a, b):
    return lax.dot_general(
        a.astype(BF16), b.astype(BF16), (((1,), (1,)), ((), ())), preferred_element_type=F32
    )


def silu(v):
    return v / (1.0 + jnp.exp(-v))


def spread_kernel(x_ref, rim_ref, out_ref):
    block = x_ref[...]
    rim = rim_ref[rim_ref.shape[0] - TAIL :, :]
    for part in range(out_ref.shape[0]):
        out_ref[part, 0:TAIL, :] = rim
        out_ref[part, TAIL:, :] = block


def stage_kernel(w_ref, out_ref, sem):
    copy = pltpu.make_async_copy(w_ref, out_ref, sem)
    copy.start()
    copy.wait()


def unit_lower_inverses(lowers, rows_at, cols_at):
    rows = lowers[0].shape[0]
    eye = (rows_at == cols_at).astype(F32)

    apart = rows_at ^ cols_at

    def joins(size):
        return (apart >= size) & (apart < 2 * size)

    first = joins(1)
    found = [eye - jnp.where(first, lower, 0.0) for lower in lowers]
    size = 2
    while size < rows:
        mask = joins(size)
        halfway = [mm(jnp.where(mask, lower, 0.0), t) for lower, t in zip(lowers, found)]
        found = [t - mm(t, h) for t, h in zip(found, halfway)]
        size *= 2
    return found


def chunk_kernel(
    lens_ref,
    first_ref,
    rate_ref,
    bias_ref,
    x_ref,
    w_ref,
    wr_ref,
    cw_ref,
    c_ref,
    wu_ref,
    ratio_ref,
    q_ref,
    k_ref,
    follow_ref,
    wide,
    ext,
):
    parts, rows, width = x_ref.shape
    rows = rows - TAIL
    dk = cw_ref.shape[2] // 4
    for part in range(parts):
        wide[:, part * width : (part + 1) * width] = x_ref[part]
    mixed = jnp.dot(wide[...], w_ref[:, : 4 * dk], preferred_element_type=F32)
    ext[...] = mixed.astype(BF16).astype(F32)
    rates = mm_nt(wide[TAIL : TAIL + rows, :], wr_ref[...]).astype(BF16).astype(F32)
    first = first_ref[0]
    pos = first + lax.broadcasted_iota(jnp.int32, (rows, 1), 0)
    start = jnp.zeros((rows, 1), jnp.int32)
    bound = jnp.int32(0)
    for i in range(lens_ref.shape[0] - 1):
        bound = bound + lens_ref[i]
        start = jnp.where(pos >= bound, bound, start)

    conv = cw_ref[0] * ext[TAIL : TAIL + rows, :]
    for j in range(1, 4):
        keep = (pos - j >= start).astype(F32)
        conv = conv + cw_ref[j] * (ext[TAIL - j : TAIL - j + rows, :] * keep)
    conv = silu(conv)
    q = conv[:, :dk]
    k = conv[:, dk : 2 * dk]
    q = q * (lax.rsqrt(jnp.sum(q * q, -1, keepdims=True) + 1e-6) * (1.0 / math.sqrt(dk)))
    k = k * lax.rsqrt(jnp.sum(k * k, -1, keepdims=True) + 1e-6)
    qb = q.astype(BF16)
    kb = k.astype(BF16)

    betas = 1.0 / (1.0 + jnp.exp(-rates[:, 0:2]))
    lane2 = lax.broadcasted_iota(jnp.int32, (1, 2), 1)
    bias = jnp.where(lane2 == 0, bias_ref[0], bias_ref[1])
    decay = jnp.where(lane2 == 0, rate_ref[0], rate_ref[1])
    a_in = rates[:, 2:4] + bias
    steps = -decay * (jnp.maximum(a_in, 0.0) + jnp.log1p(jnp.exp(-jnp.abs(a_in))))

    rows_at = lax.broadcasted_iota(jnp.int32, (rows, rows), 0)
    cols_at = lax.broadcasted_iota(jnp.int32, (rows, rows), 1)
    lower = rows_at >= cols_at
    tri = lower.astype(BF16)
    lanes = lax.broadcasted_iota(jnp.int32, (1, dk), 1)
    padded = jnp.where(lanes == 0, steps[:, 0:1], jnp.where(lanes == 1, steps[:, 1:2], 0.0))
    p1 = padded.astype(BF16)
    r1 = padded - p1.astype(F32)
    p2 = r1.astype(BF16)
    p3 = (r1 - p2.astype(F32)).astype(BF16)
    cumul = (
        jnp.dot(tri, p1, preferred_element_type=F32)
        + jnp.dot(tri, p2, preferred_element_type=F32)
        + jnp.dot(tri, p3, preferred_element_type=F32)
    )
    cumul_t = jnp.transpose(cumul)

    visible = lower & (cols_at + first >= start)
    gram = mm_nt(kb, kb)
    last_start = start[rows - 1 : rows, :]
    carries = (start < first).astype(F32)
    in_tail = (pos >= last_start).astype(F32)
    q_ref[...] = qb
    k_ref[...] = kb

    half = rows // 2
    diagonals, below, rights = [], [], []
    for h in range(2):
        col = cumul[:, h : h + 1]
        beta = betas[:, h : h + 1]
        gamma = jnp.exp(col) * carries
        differ = col - cumul_t[h : h + 1, :]
        ratio = jnp.where(visible, jnp.exp(jnp.where(visible, differ, 0.0)), 0.0)
        ratio_ref[h] = ratio
        weighed = beta * ratio * gram
        diagonals.append(weighed[:half, :half])
        diagonals.append(weighed[half:, half:])
        below.append(weighed[half:, :half])
        value = conv[:, (2 + h) * dk : (3 + h) * dk]
        rights.append(jnp.concatenate([(beta * gamma) * k, beta * value], axis=1))
        follow_ref[h] = (gamma * q).astype(BF16)
    inverses = unit_lower_inverses(
        diagonals, rows_at[:half, :half], cols_at[:half, :half]
    )
    tops = [mm(inverses[2 * h], rights[h][:half]) for h in range(2)]
    reduced = [rights[h][half:] - mm(below[h], tops[h]) for h in range(2)]
    bottoms = [mm(inverses[2 * h + 1], reduced[h]) for h in range(2)]
    square = lax.broadcasted_iota(jnp.int32, (dk, 2 * dk), 0)
    across = lax.broadcasted_iota(jnp.int32, (dk, 2 * dk), 1)
    for h in range(2):
        col = cumul[:, h : h + 1]
        last = col[rows - 1 : rows, :]
        k_tail = jnp.transpose(k * (jnp.exp(last - col) * in_tail)).astype(BF16)
        wu = jnp.concatenate([tops[h], bottoms[h]], axis=0).astype(BF16)
        wu_ref[h] = wu
        made = jnp.dot(k_tail, wu, preferred_element_type=F32)
        gamma_last = jnp.exp(last) * carries[rows - 1 : rows, :]
        c_ref[h] = (
            jnp.where(square == across, gamma_last, 0.0) + jnp.where(across < dk, -made, made)
        ).astype(BF16)


def detail_kernel(
    x_ref, w_ref, wu_ref, ratio_ref, q_ref, k_ref, follow_ref, gain_ref, m_ref, o_ref, gate_ref, wide
):
    parts, rows, width = x_ref.shape
    rows = rows - TAIL
    dk = gain_ref.shape[1]
    cross = mm_nt(q_ref[...], k_ref[...])
    for h in range(2):
        both = mm(cross * ratio_ref[h], wu_ref[h])
        m_ref[h] = (follow_ref[h].astype(F32) - both[:, :dk]).astype(BF16)
        o_ref[h] = both[:, dk:]
    for part in range(parts):
        wide[:, part * width : (part + 1) * width] = x_ref[part, TAIL : TAIL + rows, :]
    z = jnp.dot(wide[...], w_ref[:, 4 * dk :], preferred_element_type=F32)
    gate = silu(z.astype(BF16).astype(F32))
    for h in range(2):
        gate_ref[:, h * dk : (h + 1) * dk] = gate[:, h * dk : (h + 1) * dk] * gain_ref[...]


def compose(late, early):
    dk = late.shape[0]
    made = jnp.dot(late[:, :dk], early, preferred_element_type=F32)
    across = lax.broadcasted_iota(jnp.int32, made.shape, 1)
    return made + jnp.where(across < dk, 0.0, late.astype(F32))


def compose_kernel(late_ref, early_ref, out_ref):
    for h in range(2):
        out_ref[h] = compose(late_ref[h], early_ref[h]).astype(BF16)


def advance(summary, state):
    dk = summary.shape[0]
    moved = jnp.dot(summary[:, :dk], state, preferred_element_type=F32)
    return (moved + summary[:, dk:].astype(F32)).astype(BF16)


def enter_kernel(near_ref, far_ref, out_ref):
    for h in range(2):
        out_ref[h] = advance(near_ref[h], far_ref[h])


def finish_kernel(
    made_ref, given_ref, first_half_ref, m_ref, o_ref, gate_ref, w_ref, out_ref
):
    dk = m_ref.shape[2]
    parts, _, width = out_ref.shape
    sides = []
    for h in range(2):
        state = given_ref[h] + advance(first_half_ref[h], made_ref[h])
        rec = o_ref[h] + jnp.dot(m_ref[h], state, preferred_element_type=F32)
        scale = lax.rsqrt(jnp.mean(rec * rec, -1, keepdims=True) + 1e-6)
        sides.append((rec * scale * gate_ref[:, h * dk : (h + 1) * dk]).astype(BF16))
    normed = jnp.concatenate(sides, axis=1)
    share = jnp.dot(normed, w_ref[...], preferred_element_type=F32).astype(BF16)
    for part in range(parts):
        out_ref[part] = share[:, part * width : (part + 1) * width]


def vmem():
    return pl.BlockSpec(memory_space=pltpu.VMEM)


def smem():
    return pl.BlockSpec(memory_space=pltpu.SMEM)


def params():
    return pltpu.CompilerParams(vmem_limit_bytes=VMEM_LIMIT)


def shifted(array, by):
    peers = lax.axis_size("context")
    return lax.ppermute(array, "context", [(i, i + by) for i in range(peers - by)])


def within_chip(array, source):
    peers = lax.axis_size("context")
    pairs = [(i + source, i + 1 - source) for i in range(0, peers, 2)]
    return lax.ppermute(array, "context", pairs)


def over_chips(array, by):
    peers = lax.axis_size("context")
    pairs = [(i, i + 2 * by) for i in range(1, peers - 2 * by, 2)]
    return lax.ppermute(array, "context", pairs)


def local(
    hidden,
    proj_qkvz,
    proj_rates,
    conv_weight,
    decay_rate,
    step_bias,
    norm_gain,
    proj_out,
    doc_lengths,
):
    rows, width = hidden.shape
    dk = norm_gain.shape[0]
    peers = lax.axis_size("tensor")
    first = (lax.axis_index("context") * rows).astype(jnp.int32).reshape(1)
    shape = jax.ShapeDtypeStruct

    tail = shifted(hidden, 1)
    spread = pl.pallas_call(
        spread_kernel,
        out_shape=shape((peers, TAIL + rows, width), BF16),
        in_specs=[vmem()] * 2,
        out_specs=vmem(),
        compiler_params=params(),
    )(hidden, tail)
    staged = pl.pallas_call(
        stage_kernel,
        out_shape=shape(proj_qkvz.shape, BF16),
        in_specs=[pl.BlockSpec(memory_space=pl.ANY)],
        out_specs=vmem(),
        scratch_shapes=[pltpu.SemaphoreType.DMA],
        compiler_params=params(),
    )(proj_qkvz)
    spread, staged, first = lax.optimization_barrier((spread, staged, first))
    gathered = lax.all_to_all(spread, "tensor", 0, 0, tiled=True)

    summary, inner, ratio, query, key, reach = pl.pallas_call(
        chunk_kernel,
        out_shape=(
            shape((2, dk, 2 * dk), BF16),
            shape((2, rows, 2 * dk), BF16),
            shape((2, rows, rows), F32),
            shape((rows, dk), BF16),
            shape((rows, dk), BF16),
            shape((2, rows, dk), BF16),
        ),
        in_specs=[smem()] * 4 + [vmem()] * 4,
        out_specs=(vmem(),) * 6,
        scratch_shapes=[
            pltpu.VMEM((rows + TAIL, peers * width), BF16),
            pltpu.VMEM((rows + TAIL, 4 * dk), F32),
        ],
        compiler_params=params(),
    )(
        doc_lengths,
        first,
        decay_rate,
        step_bias,
        gathered,
        staged,
        proj_rates.T,
        conv_weight,
    )
    follow, own, gate = pl.pallas_call(
        detail_kernel,
        out_shape=(
            shape((2, rows, dk), BF16),
            shape((2, rows, dk), F32),
            shape((rows, 2 * dk), F32),
        ),
        in_specs=[vmem()] * 8,
        out_specs=(vmem(),) * 3,
        scratch_shapes=[pltpu.VMEM((rows, peers * width), BF16)],
        compiler_params=params(),
    )(gathered, staged, inner, ratio, query, key, reach, norm_gain.reshape(1, dk))

    def small(kernel, columns, *arrays):
        return pl.pallas_call(
            kernel,
            out_shape=shape((2, dk, columns), BF16),
            in_specs=[vmem()] * len(arrays),
            out_specs=vmem(),
            compiler_params=params(),
        )(*arrays)

    first_half = within_chip(summary, 0)
    first_half, follow, own, gate = lax.optimization_barrier((first_half, follow, own, gate))
    chip = small(compose_kernel, 2 * dk, summary, first_half)
    window = small(compose_kernel, 2 * dk, over_chips(chip, 1), over_chips(chip, 2))
    window = small(compose_kernel, 2 * dk, window, over_chips(window, 2))
    made = small(enter_kernel, dk, window, over_chips(window[:, :, dk:], 4))
    given = within_chip(made, 1)

    share = pl.pallas_call(
        finish_kernel,
        out_shape=shape((peers, rows, width), BF16),
        in_specs=[vmem()] * 7,
        out_specs=vmem(),
        compiler_params=params(),
    )(made, given, first_half, follow, own, gate, proj_out)
    shares = lax.all_to_all(share, "tensor", 0, 0, tiled=True)
    return jnp.sum(shares.astype(F32), axis=0).astype(BF16)


def solution(mesh):
    placed = (
        P("context", "tensor"),
        P(None, "tensor"),
        P(None, "tensor"),
        P(None, "tensor", None),
        P("tensor"),
        P("tensor"),
        P(),
        P("tensor", None),
        P(),
    )
    return jax.shard_map(
        local, mesh=mesh, in_specs=placed, out_specs=P("context", "tensor"), check_vma=False
    )
```

```python
import functools
import math

import jax
import jax.numpy as jnp
from jax import lax
from jax.experimental import pallas as pl
from jax.experimental.pallas import tpu as pltpu
from jax.sharding import PartitionSpec as P

F32 = jnp.float32
BF16 = jnp.bfloat16
TAIL = 16
VMEM_LIMIT = 48 * 1024 * 1024


def mm(a, b):
    return jnp.dot(a.astype(BF16), b.astype(BF16), preferred_element_type=F32)


def mm_nt(a, b):
    return lax.dot_general(
        a.astype(BF16), b.astype(BF16), (((1,), (1,)), ((), ())), preferred_element_type=F32
    )


def silu(v):
    return v / (1.0 + jnp.exp(-v))


def spread_kernel(x_ref, rim_ref, out_ref):
    block = x_ref[...]
    rim = rim_ref[rim_ref.shape[0] - TAIL :, :]
    for part in range(out_ref.shape[0]):
        out_ref[part, 0:TAIL, :] = rim
        out_ref[part, TAIL:, :] = block


def stage_kernel(w_ref, out_ref, sem):
    copy = pltpu.make_async_copy(w_ref, out_ref, sem)
    copy.start()
    copy.wait()


def unit_lower_inverses(lowers, rows_at, cols_at):
    rows = lowers[0].shape[0]
    eye = (rows_at == cols_at).astype(F32)

    apart = rows_at ^ cols_at

    def joins(size):
        return (apart >= size) & (apart < 2 * size)

    first = joins(1)
    found = [eye - jnp.where(first, lower, 0.0) for lower in lowers]
    size = 2
    while size < rows:
        mask = joins(size)
        halfway = [mm(jnp.where(mask, lower, 0.0), t) for lower, t in zip(lowers, found)]
        found = [t - mm(t, h) for t, h in zip(found, halfway)]
        size *= 2
    return found


def chunk_kernel(
    lens_ref,
    first_ref,
    rate_ref,
    bias_ref,
    x_ref,
    w_ref,
    wr_ref,
    cw_ref,
    c_ref,
    wu_ref,
    ratio_ref,
    q_ref,
    k_ref,
    follow_ref,
    wide,
    ext,
):
    parts, rows, width = x_ref.shape
    rows = rows - TAIL
    dk = cw_ref.shape[2] // 4
    for part in range(parts):
        wide[:, part * width : (part + 1) * width] = x_ref[part]
    mixed = jnp.dot(wide[...], w_ref[:, : 4 * dk], preferred_element_type=F32)
    ext[...] = mixed.astype(BF16).astype(F32)
    rates = mm_nt(wide[TAIL : TAIL + rows, :], wr_ref[...]).astype(BF16).astype(F32)
    first = first_ref[0]
    pos = first + lax.broadcasted_iota(jnp.int32, (rows, 1), 0)
    start = jnp.zeros((rows, 1), jnp.int32)
    bound = jnp.int32(0)
    for i in range(lens_ref.shape[0] - 1):
        bound = bound + lens_ref[i]
        start = jnp.where(pos >= bound, bound, start)

    conv = cw_ref[0] * ext[TAIL : TAIL + rows, :]
    for j in range(1, 4):
        keep = (pos - j >= start).astype(F32)
        conv = conv + cw_ref[j] * (ext[TAIL - j : TAIL - j + rows, :] * keep)
    conv = silu(conv)
    q = conv[:, :dk]
    k = conv[:, dk : 2 * dk]
    q = q * (lax.rsqrt(jnp.sum(q * q, -1, keepdims=True) + 1e-6) * (1.0 / math.sqrt(dk)))
    k = k * lax.rsqrt(jnp.sum(k * k, -1, keepdims=True) + 1e-6)
    qb = q.astype(BF16)
    kb = k.astype(BF16)

    betas = 1.0 / (1.0 + jnp.exp(-rates[:, 0:2]))
    lane2 = lax.broadcasted_iota(jnp.int32, (1, 2), 1)
    bias = jnp.where(lane2 == 0, bias_ref[0], bias_ref[1])
    decay = jnp.where(lane2 == 0, rate_ref[0], rate_ref[1])
    a_in = rates[:, 2:4] + bias
    steps = -decay * (jnp.maximum(a_in, 0.0) + jnp.log1p(jnp.exp(-jnp.abs(a_in))))

    rows_at = lax.broadcasted_iota(jnp.int32, (rows, rows), 0)
    cols_at = lax.broadcasted_iota(jnp.int32, (rows, rows), 1)
    lower = rows_at >= cols_at
    tri = lower.astype(BF16)
    lanes = lax.broadcasted_iota(jnp.int32, (1, dk), 1)
    padded = jnp.where(lanes == 0, steps[:, 0:1], jnp.where(lanes == 1, steps[:, 1:2], 0.0))
    p1 = padded.astype(BF16)
    r1 = padded - p1.astype(F32)
    p2 = r1.astype(BF16)
    p3 = (r1 - p2.astype(F32)).astype(BF16)
    cumul = (
        jnp.dot(tri, p1, preferred_element_type=F32)
        + jnp.dot(tri, p2, preferred_element_type=F32)
        + jnp.dot(tri, p3, preferred_element_type=F32)
    )
    cumul_t = jnp.transpose(cumul)

    visible = lower & (cols_at + first >= start)
    gram = mm_nt(kb, kb)
    last_start = start[rows - 1 : rows, :]
    carries = (start < first).astype(F32)
    in_tail = (pos >= last_start).astype(F32)
    q_ref[...] = qb
    k_ref[...] = kb

    half = rows // 2
    diagonals, below, rights = [], [], []
    for h in range(2):
        col = cumul[:, h : h + 1]
        beta = betas[:, h : h + 1]
        gamma = jnp.exp(col) * carries
        differ = col - cumul_t[h : h + 1, :]
        ratio = jnp.where(visible, jnp.exp(jnp.where(visible, differ, 0.0)), 0.0)
        ratio_ref[h] = ratio
        weighed = beta * ratio * gram
        diagonals.append(weighed[:half, :half])
        diagonals.append(weighed[half:, half:])
        below.append(weighed[half:, :half])
        value = conv[:, (2 + h) * dk : (3 + h) * dk]
        rights.append(jnp.concatenate([(beta * gamma) * k, beta * value], axis=1))
        follow_ref[h] = (gamma * q).astype(BF16)
    inverses = unit_lower_inverses(
        diagonals, rows_at[:half, :half], cols_at[:half, :half]
    )
    tops = [mm(inverses[2 * h], rights[h][:half]) for h in range(2)]
    reduced = [rights[h][half:] - mm(below[h], tops[h]) for h in range(2)]
    bottoms = [mm(inverses[2 * h + 1], reduced[h]) for h in range(2)]
    square = lax.broadcasted_iota(jnp.int32, (dk, 2 * dk), 0)
    across = lax.broadcasted_iota(jnp.int32, (dk, 2 * dk), 1)
    for h in range(2):
        col = cumul[:, h : h + 1]
        last = col[rows - 1 : rows, :]
        k_tail = jnp.transpose(k * (jnp.exp(last - col) * in_tail)).astype(BF16)
        wu = jnp.concatenate([tops[h], bottoms[h]], axis=0).astype(BF16)
        wu_ref[h] = wu
        made = jnp.dot(k_tail, wu, preferred_element_type=F32)
        gamma_last = jnp.exp(last) * carries[rows - 1 : rows, :]
        c_ref[h] = (
            jnp.where(square == across, gamma_last, 0.0) + jnp.where(across < dk, -made, made)
        ).astype(BF16)


def detail_kernel(
    x_ref, w_ref, wu_ref, ratio_ref, q_ref, k_ref, follow_ref, gain_ref, m_ref, o_ref, gate_ref, wide
):
    parts, rows, width = x_ref.shape
    rows = rows - TAIL
    dk = gain_ref.shape[1]
    cross = mm_nt(q_ref[...], k_ref[...])
    for h in range(2):
        both = mm(cross * ratio_ref[h], wu_ref[h])
        m_ref[h] = (follow_ref[h].astype(F32) - both[:, :dk]).astype(BF16)
        o_ref[h] = both[:, dk:]
    for part in range(parts):
        wide[:, part * width : (part + 1) * width] = x_ref[part, TAIL : TAIL + rows, :]
    z = jnp.dot(wide[...], w_ref[:, 4 * dk :], preferred_element_type=F32)
    gate = silu(z.astype(BF16).astype(F32))
    for h in range(2):
        gate_ref[:, h * dk : (h + 1) * dk] = gate[:, h * dk : (h + 1) * dk] * gain_ref[...]


def compose(late, early):
    dk = late.shape[0]
    made = jnp.dot(late[:, :dk], early, preferred_element_type=F32)
    across = lax.broadcasted_iota(jnp.int32, made.shape, 1)
    return made + jnp.where(across < dk, 0.0, late.astype(F32))


def compose_kernel(late_ref, early_ref, out_ref):
    for h in range(2):
        out_ref[h] = compose(late_ref[h], early_ref[h]).astype(BF16)


def advance(summary, state):
    dk = summary.shape[0]
    moved = jnp.dot(summary[:, :dk], state, preferred_element_type=F32)
    return (moved + summary[:, dk:].astype(F32)).astype(BF16)


def enter_kernel(near_ref, far_ref, out_ref):
    for h in range(2):
        out_ref[h] = advance(near_ref[h], far_ref[h])


def finish_kernel(
    made_ref, given_ref, first_half_ref, m_ref, o_ref, gate_ref, w_ref, out_ref
):
    dk = m_ref.shape[2]
    parts, _, width = out_ref.shape
    sides = []
    for h in range(2):
        state = given_ref[h] + advance(first_half_ref[h], made_ref[h])
        rec = o_ref[h] + jnp.dot(m_ref[h], state, preferred_element_type=F32)
        scale = lax.rsqrt(jnp.mean(rec * rec, -1, keepdims=True) + 1e-6)
        sides.append((rec * scale * gate_ref[:, h * dk : (h + 1) * dk]).astype(BF16))
    normed = jnp.concatenate(sides, axis=1)
    share = jnp.dot(normed, w_ref[...], preferred_element_type=F32).astype(BF16)
    for part in range(parts):
        out_ref[part] = share[:, part * width : (part + 1) * width]


def sum_kernel(shares_ref, out_ref):
    total = shares_ref[0].astype(F32)
    for part in range(1, shares_ref.shape[0]):
        total = total + shares_ref[part].astype(F32)
    out_ref[...] = total.astype(BF16)


def vmem():
    return pl.BlockSpec(memory_space=pltpu.VMEM)


def smem():
    return pl.BlockSpec(memory_space=pltpu.SMEM)


def params():
    return pltpu.CompilerParams(vmem_limit_bytes=VMEM_LIMIT)


def shifted(array, by):
    peers = lax.axis_size("context")
    return lax.ppermute(array, "context", [(i, i + by) for i in range(peers - by)])


def within_chip(array, source):
    peers = lax.axis_size("context")
    pairs = [(i + source, i + 1 - source) for i in range(0, peers, 2)]
    return lax.ppermute(array, "context", pairs)


def over_chips(array, by):
    peers = lax.axis_size("context")
    pairs = [(i, i + 2 * by) for i in range(1, peers - 2 * by, 2)]
    return lax.ppermute(array, "context", pairs)


def local(
    hidden,
    proj_qkvz,
    proj_rates,
    conv_weight,
    decay_rate,
    step_bias,
    norm_gain,
    proj_out,
    doc_lengths,
):
    rows, width = hidden.shape
    dk = norm_gain.shape[0]
    peers = lax.axis_size("tensor")
    first = (lax.axis_index("context") * rows).astype(jnp.int32).reshape(1)
    shape = jax.ShapeDtypeStruct

    tail = shifted(hidden, 1)
    spread = pl.pallas_call(
        spread_kernel,
        out_shape=shape((peers, TAIL + rows, width), BF16),
        in_specs=[vmem()] * 2,
        out_specs=vmem(),
        compiler_params=params(),
    )(hidden, tail)
    staged = pl.pallas_call(
        stage_kernel,
        out_shape=shape(proj_qkvz.shape, BF16),
        in_specs=[pl.BlockSpec(memory_space=pl.ANY)],
        out_specs=vmem(),
        scratch_shapes=[pltpu.SemaphoreType.DMA],
        compiler_params=params(),
    )(proj_qkvz)
    spread, staged, first = lax.optimization_barrier((spread, staged, first))
    gathered = lax.all_to_all(spread, "tensor", 0, 0, tiled=True)

    summary, inner, ratio, query, key, reach = pl.pallas_call(
        chunk_kernel,
        out_shape=(
            shape((2, dk, 2 * dk), BF16),
            shape((2, rows, 2 * dk), BF16),
            shape((2, rows, rows), F32),
            shape((rows, dk), BF16),
            shape((rows, dk), BF16),
            shape((2, rows, dk), BF16),
        ),
        in_specs=[smem()] * 4 + [vmem()] * 4,
        out_specs=(vmem(),) * 6,
        scratch_shapes=[
            pltpu.VMEM((rows + TAIL, peers * width), BF16),
            pltpu.VMEM((rows + TAIL, 4 * dk), F32),
        ],
        compiler_params=params(),
    )(
        doc_lengths,
        first,
        decay_rate,
        step_bias,
        gathered,
        staged,
        proj_rates.T,
        conv_weight,
    )
    follow, own, gate = pl.pallas_call(
        detail_kernel,
        out_shape=(
            shape((2, rows, dk), BF16),
            shape((2, rows, dk), F32),
            shape((rows, 2 * dk), F32),
        ),
        in_specs=[vmem()] * 8,
        out_specs=(vmem(),) * 3,
        scratch_shapes=[pltpu.VMEM((rows, peers * width), BF16)],
        compiler_params=params(),
    )(gathered, staged, inner, ratio, query, key, reach, norm_gain.reshape(1, dk))

    def small(kernel, columns, *arrays):
        return pl.pallas_call(
            kernel,
            out_shape=shape((2, dk, columns), BF16),
            in_specs=[vmem()] * len(arrays),
            out_specs=vmem(),
            compiler_params=params(),
        )(*arrays)

    first_half = within_chip(summary, 0)
    first_half, follow, own, gate = lax.optimization_barrier((first_half, follow, own, gate))
    chip = small(compose_kernel, 2 * dk, summary, first_half)
    window = small(compose_kernel, 2 * dk, over_chips(chip, 1), over_chips(chip, 2))
    window = small(compose_kernel, 2 * dk, window, over_chips(window, 2))
    made = small(enter_kernel, dk, window, over_chips(window[:, :, dk:], 4))
    given = within_chip(made, 1)

    share = pl.pallas_call(
        finish_kernel,
        out_shape=shape((peers, rows, width), BF16),
        in_specs=[vmem()] * 7,
        out_specs=vmem(),
        compiler_params=params(),
    )(made, given, first_half, follow, own, gate, proj_out)
    shares = lax.all_to_all(share, "tensor", 0, 0, tiled=True)
    return pl.pallas_call(
        sum_kernel,
        out_shape=shape((rows, width), BF16),
        in_specs=[vmem()],
        out_specs=vmem(),
        compiler_params=params(),
    )(shares)


def solution(mesh):
    placed = (
        P("context", "tensor"),
        P(None, "tensor"),
        P(None, "tensor"),
        P(None, "tensor", None),
        P("tensor"),
        P("tensor"),
        P(),
        P("tensor", None),
        P(),
    )
    return jax.shard_map(
        local, mesh=mesh, in_specs=placed, out_specs=P("context", "tensor"), check_vma=False
    )
```
